32 devices in a mesh: lon: 16 (over z, y, x), lat: 2 (over core).
Axes of the slice: x: 2, y: 2, z: 4, core: 2. Of those that a mesh axis runs over, the one named last changes fastest.
Arguments:
- grid_fields: float32 [48, 1280, 2560], P(None, 'lat', 'lon'), may hold values from -6 to 6
- legendre: bfloat16 [640, 1280, 1281], P('lon', 'lat'), may hold values from -12 to 12
- pair_order: int32 [640], replicated, may hold values from 0 to 639, each once
Outputs:
- spectral: float32 [48, 640, 2, 1281], P('lat', 'lon')
The draws below stay inside these ranges and needn't reach their ends.
Inputs may be any that keep to these rules, and one draw needn't show every extreme that they name: A permutation; slot s holds wavenumbers pair_order[s] and 1279 - pair_order[s].
All inputs are finite; a program needn't handle non-finite values.
Results may differ from the reference program's by a relative error of at most 0.0029.
Values may be sent and summed in bfloat16 or wider, within the bound.
A program may use at most 320 MiB of HBM per device.

```python
import jax
import jax.numpy as jnp
from jax import lax

NLON = 2560
NLAT = 1280
M = 1280
FIELDS = 48
NPAIR = 640
NROW = 1281


def shard_levels(key, extent, cuts, smallest, high):
    loudness = 1.0
    for position, shards_of in cuts:
        draws = jax.random.uniform(jax.random.fold_in(jax.random.fold_in(key, 6), position), (shards_of,), jnp.float32, smallest / len(cuts), high / len(cuts))
        loudness = loudness * jnp.repeat(jnp.exp(draws), extent[position] // shards_of).reshape((-1,) + (1,) * (len(extent) - 1 - position))
    return loudness


def noise(own_key, dims, deviation, limit, shards=(), kind=jnp.bfloat16):
    loudness = shard_levels(own_key, dims, shards, -0.22, 0.18) if shards else 1.0
    entries = jax.random.normal(own_key, dims, jnp.float32) * deviation * loudness
    return jnp.minimum(jnp.maximum(entries, -limit), limit).astype(kind)


def setup_inputs(seed: int = 0) -> dict:
    arg_keys = jax.random.split(jax.random.key(seed), 4)
    return {
        "grid_fields": noise(arg_keys[0], (FIELDS, NLAT, NLON), 1.0, 6.0, ((1, 2), (2, 16)), jnp.float32),
        "legendre": noise(arg_keys[1], (NPAIR, NLAT, NROW), 2.0, 12.0, ((0, 16), (1, 2))),
        "pair_order": jax.random.permutation(arg_keys[2], NPAIR).astype(jnp.int32),
    }


def reference(grid_fields, legendre, pair_order):
    spectrum = jnp.fft.rfft(grid_fields, axis=-1)[..., :M] / NLON
    real_part = jnp.real(spectrum)
    imag_part = jnp.imag(spectrum)
    lower_wave = pair_order
    upper_wave = M - 1 - pair_order
    fourier = jnp.stack([real_part[..., lower_wave], imag_part[..., lower_wave],
                         real_part[..., upper_wave], imag_part[..., upper_wave]], axis=-1).astype(jnp.bfloat16)
    by_pair = jnp.transpose(fourier, (2, 0, 1, 3))
    row_index = jnp.arange(M + 1, dtype=jnp.int32)

    def one_pair(items):
        table, coef_block, which_pair = items
        table_wide = table.astype(jnp.float32)
        coef_wide = coef_block.astype(jnp.float32)
        lower_sum = jnp.einsum("fjc,jr->fcr", coef_wide[..., 0:2], table_wide, precision=lax.Precision.HIGHEST)
        upper_sum = jnp.einsum("fjc,jr->fcr", coef_wide[..., 2:4], table_wide, precision=lax.Precision.HIGHEST)
        return jnp.where((row_index >= M - which_pair)[None, None, :], upper_sum, lower_sum)

    result = lax.map(one_pair, (legendre, by_pair, pair_order), batch_size=16)
    return jnp.transpose(result, (1, 0, 2, 3))
```

```python
import math

import jax
import jax.numpy as jnp
from jax import lax
from jax.sharding import PartitionSpec as P

NLON = 2560
M = 1280
NPAIR = 640
WIRE = jnp.float16
WIRE_SCALE = 8192.0
FINE = 64


def basis(pair_order):
    upper_wave = M - 1 - pair_order
    waves = jnp.stack([pair_order, pair_order, upper_wave, upper_wave], axis=1).reshape(-1)
    shift = (jnp.arange(4 * NPAIR, dtype=jnp.int32) % 2) * (NLON // 4)
    coarse = (waves[:, None] * (FINE * jnp.arange(NLON // FINE, dtype=jnp.int32))[None, :] + shift[:, None]) % NLON
    fine = waves[:, None] * jnp.arange(FINE, dtype=jnp.int32)[None, :] % NLON
    unit = 2.0 * math.pi / NLON
    coarse = coarse.astype(jnp.float32) * unit
    fine = fine.astype(jnp.float32) * unit
    norm = 1.0 / (NLON * WIRE_SCALE)
    ca, sa = jnp.cos(coarse) * norm, jnp.sin(coarse) * norm
    cb, sb = jnp.cos(fine), jnp.sin(fine)
    ca, sa, cb, sb = lax.optimization_barrier((ca, sa, cb, sb))
    table = ca[:, :, None] * cb[:, None, :] - sa[:, :, None] * sb[:, None, :]
    return table.reshape(4 * NPAIR, NLON)


def on_device(grid_fields, legendre, pair_order):
    field_count, band, lon_local = grid_fields.shape
    slots = legendre.shape[0]
    devices = lax.axis_size("lon")
    half_rows = M // 2 + 1
    split_f = math.gcd(field_count, devices)
    split_l = devices // split_f
    chunks = field_count // split_f
    part = band // split_l

    by_lon = jnp.transpose(grid_fields, (0, 2, 1))
    received = []
    for i in range(chunks):
        own = by_lon[i * split_f:(i + 1) * split_f]
        own = (own * WIRE_SCALE).astype(WIRE)
        own = own.reshape(split_f, lon_local, split_l, part).transpose(0, 2, 1, 3)
        own = own.reshape(devices, lon_local, part)
        received.append(lax.all_to_all(own, "lon", split_axis=0, concat_axis=0, tiled=True))
    table = basis(pair_order)
    waves = []
    for i in range(chunks):
        rows = received[i].reshape(NLON, part).astype(jnp.float32)
        coef = jnp.dot(table, rows, precision=lax.Precision.HIGH, preferred_element_type=jnp.float32)
        fourier = coef.astype(jnp.bfloat16).reshape(devices, slots * 4, part)
        owned = lax.all_to_all(fourier, "lon", split_axis=0, concat_axis=0, tiled=True)
        owned = owned.reshape(split_f, split_l, slots * 4, part).transpose(0, 2, 1, 3)
        waves.append(owned.reshape(split_f, slots, 4, band))
    waves_local = jnp.concatenate(waves, axis=0)

    own_pairs = lax.dynamic_slice_in_dim(pair_order, lax.axis_index("lon") * slots, slots)
    row_index = jnp.arange(half_rows, M + 1, dtype=jnp.int32)
    use_upper = row_index[None, :] >= (M - own_pairs)[:, None]
    turned = lax.optimization_barrier(jnp.transpose(legendre, (0, 2, 1)))
    lower_table = turned[:, :half_rows]
    upper_table = turned[:, half_rows:]
    lower = jnp.transpose(waves_local[:, :, 0:2], (1, 0, 2, 3)).reshape(slots, field_count * 2, band)
    upper = jnp.transpose(waves_local[:, :, 2:4], (1, 0, 2, 3)).reshape(slots, field_count * 2, band)

    def sums(w, t):
        return lax.dot_general(w, t, (((2,), (2,)), ((0,), (0,))), preferred_element_type=jnp.float32)

    leading = sums(lower, lower_table)
    trailing = jnp.where(use_upper[:, None, :], sums(upper, upper_table), sums(lower, upper_table))
    totals = jnp.concatenate([leading, trailing], axis=2)
    totals = totals.reshape(slots, field_count, 2, M + 1).transpose(1, 0, 2, 3)
    return lax.psum_scatter(totals, "lat", scatter_dimension=0, tiled=True)


def solution(mesh):
    in_specs = (P(None, "lat", "lon"), P("lon", "lat", None), P())
    out_specs = P("lat", "lon", None, None)
    return jax.shard_map(
        on_device, mesh=mesh, in_specs=in_specs, out_specs=out_specs, check_vma=False
    )
```
